32 devices in a mesh: groups: 2 (over x), ctx: 8 (over z, y), head: 2 (over core).
Axes of the slice: x: 2, y: 2, z: 4, core: 2. Of those that a mesh axis runs over, the one named last changes fastest.
Arguments:
- q_prefill: bfloat16 [2048, 64, 576], P(('groups', 'ctx'), 'head'), parts along dimension 0, may hold values from -300 to 300
- kv_raw: bfloat16 [2048, 576], P(('groups', 'ctx')), parts along dimension 0, may hold values from -6 to 6
- kv_gain: float32 [512], replicated, may hold values from 0.1 to 1.9
- block_mask: int32 [16, 8], P('groups'), parts along dimension 0, may hold values from 0 to 1, as said below
- owner: int32 [16], P('groups'), parts along dimension 0, may hold values from 0 to 7, as said below
- decode_len: int32 [32], P('groups'), parts along dimension 0, may hold values from 1 to 1024, as said below
- q_decode: bfloat16 [3, 32, 64, 576], P(None, 'groups', 'head'), parts along dimension 1, may hold values from -300 to 300
- kv_new_raw: bfloat16 [3, 32, 576], P(None, 'groups'), parts along dimension 1, may hold values from -6 to 6
Outputs:
- prefill_out: bfloat16 [2048, 64, 512], P(('groups', 'ctx'), 'head'), parts along dimension 0
- owner_cache: bfloat16 [32, 128, 576], P(('groups', 'ctx')), parts along dimension 0
- decode_out: bfloat16 [3, 32, 64, 512], P(None, 'groups', 'head'), parts along dimension 1
The draws below stay inside these ranges and needn't reach their ends.
There are 2 independent parts, one for each index of `groups`. The reference program is written for one: setup_inputs(seed, part) draws one part's arguments, and reference() takes and returns one part's arrays. A program takes and returns all parts, laid end to end along the dimension named above; an argument that names none is the same for every part. Nothing has to cross between parts.
Inputs may be any that keep to these rules, and one draw needn't show every extreme that they name: block_mask[i, j] is 0 for j > i, and 1 for j = i, for j = i - 1 and for j = 0. No owner holds more than 2 blocks; some owner holds exactly 2. `decode_len`: some row reads exactly 1024 prompt rows.
All inputs are finite; a program needn't handle non-finite values.
Results may differ from the reference program's by a relative error of at most 0.005.
The reference program's roundings to bfloat16 on the way count: a program that leaves them out, or rounds other values in their place, can miss the bound.
Values may be sent and summed in bfloat16 or wider, within the bound.
A program may use at most 128 MiB of HBM per device.

```python
import jax
import jax.numpy as jnp
from jax import lax

KVR = 512
LAT = 576
HEADS = 64
BLK = 128
STEPS = 3
CAP = 2
R = 16
TOKENS = 1024
NBLK = 8
SLOTS = 16
N_CTX = 8


def strong_rows(key, sample, row_shape):
    picks = jax.random.randint(jax.random.fold_in(key, 5), row_shape, 0, 8) == 0
    levels = 75.0 * 2.0 ** jax.random.randint(jax.random.fold_in(key, 6), row_shape, 0, 3).astype(jnp.float32)
    first = (jnp.arange(row_shape[0]) == 0).reshape((row_shape[0],) + (1,) * (len(row_shape) - 1))
    picks = picks | first
    levels = jnp.where(first, 300.0, levels)
    signs = jnp.where(jax.random.normal(jax.random.fold_in(key, 7), sample.shape, jnp.float32) >= 0.0, 1.0, -1.0)
    return jnp.where(picks, levels * signs, sample)


def draw_q_prefill(key, part):
    key = jax.random.fold_in(key, 11)
    sample = jnp.clip(jax.random.normal(jax.random.fold_in(key, 2), (TOKENS, HEADS, LAT), jnp.float32), -6.0, 6.0)
    sample = strong_rows(key, sample, (TOKENS, HEADS, 1))
    return sample.astype(jnp.bfloat16)


def draw_q_decode(key, part):
    key = jax.random.fold_in(key, 17)
    sample = jnp.clip(jax.random.normal(jax.random.fold_in(key, 2), (STEPS, R, HEADS, LAT), jnp.float32), -6.0, 6.0)
    sample = strong_rows(key, sample, (STEPS, R, HEADS, 1))
    return sample.astype(jnp.bfloat16)


def draw_block_mask(key, part):
    key = jax.random.fold_in(key, 23)
    picks = jax.random.randint(jax.random.fold_in(key, 1), (NBLK, NBLK), 0, 4) == 0
    query_side = jnp.arange(NBLK, dtype=jnp.int32)[:, None]
    key_side = jnp.arange(NBLK, dtype=jnp.int32)[None, :]
    live = (key_side == query_side) | (key_side == query_side - 1) | (key_side == 0) & (query_side >= 0) | picks & (key_side < query_side)
    return live.astype(jnp.int32)


def draw_owner(key, part):
    key = jax.random.fold_in(key, 29)
    slots = jax.random.permutation(jax.random.fold_in(key, 1), N_CTX * CAP)
    slot_owner = (slots // CAP).astype(jnp.int32)
    behind = (slot_owner != slot_owner[0]).astype(jnp.int32)
    order = jnp.argsort(behind, stable=True)
    chosen = slot_owner[order][:NBLK]
    shuffle = jax.random.permutation(jax.random.fold_in(key, 2), NBLK)
    return chosen[shuffle].astype(jnp.int32)


def draw_decode_len(key, part):
    key = jax.random.fold_in(key, 31)
    lengths = jax.random.randint(jax.random.fold_in(key, 1), (R,), 1, TOKENS + 1)
    top_row = jax.random.randint(jax.random.fold_in(key, 2), (), 0, R)
    return jnp.where(jnp.arange(R) == top_row, TOKENS, lengths).astype(jnp.int32)


def block_scale(key, extent, shards, low, high):
    loudness = 1.0
    for dim, shards_of in shards:
        draws = jax.random.uniform(jax.random.fold_in(jax.random.fold_in(key, 6), dim), (shards_of,), jnp.float32, low / len(shards), high / len(shards))
        loudness = loudness * jnp.repeat(jnp.exp(draws), extent[dim] // shards_of).reshape((-1,) + (1,) * (len(extent) - 1 - dim))
    return loudness


def scatter_about(rng, shape, spread, most, split=(), kind=jnp.bfloat16):
    result = spread * jax.random.normal(rng, shape, jnp.float32)
    if split:
        result = result * block_scale(rng, shape, split, -0.22, 0.18)
    return jnp.clip(result, -most, most).astype(kind)


def setup_inputs(seed: int = 0, part: int = 0) -> dict:
    keys = jax.random.split(jax.random.key(seed), 9)
    part_keys = jax.random.split(jax.random.fold_in(keys[8], part), 9)
    return {
        "q_prefill": draw_q_prefill(jax.random.fold_in(jax.random.fold_in(keys[8], part), 71), part),
        "kv_raw": scatter_about(part_keys[1], (TOKENS, LAT), 1.0, 6.0, ((0, 8),)),
        "kv_gain": jnp.clip(1.0 + 0.18 * jax.random.normal(keys[2], (KVR,), jnp.float32), 0.1, 1.9),
        "block_mask": draw_block_mask(jax.random.fold_in(jax.random.fold_in(keys[8], part), 71), part),
        "owner": draw_owner(jax.random.fold_in(jax.random.fold_in(keys[8], part), 71), part),
        "decode_len": draw_decode_len(jax.random.fold_in(jax.random.fold_in(keys[8], part), 71), part),
        "q_decode": draw_q_decode(jax.random.fold_in(jax.random.fold_in(keys[8], part), 71), part),
        "kv_new_raw": scatter_about(part_keys[7], (STEPS, R, LAT), 1.0, 6.0),
    }


scale_factor = 192.0 ** (-0.5)
neg_large = -1e+30

def normalize_latent(raw_rows, gain_vector, positions):
    values = raw_rows.astype(jnp.float32)
    latent_width = gain_vector.shape[0]
    main_part = values[..., :latent_width]
    main_part = main_part * lax.rsqrt(lax.optimization_barrier(jnp.mean(main_part * main_part, axis=-1, keepdims=True)) + 1e-06) * gain_vector
    rotary = values[..., latent_width:]
    half_width = rotary.shape[-1] // 2
    frequency = 10000.0 ** (-2.0 * jnp.arange(half_width, dtype=jnp.float32) / rotary.shape[-1])
    angles = positions.astype(jnp.float32)[..., None] * frequency
    cosine = jnp.cos(angles)
    sine_part = jnp.sin(angles)
    first_half = rotary[..., :half_width]
    second_half = rotary[..., half_width:]
    joined = jnp.concatenate([main_part, first_half * cosine - second_half * sine_part, first_half * sine_part + second_half * cosine], axis=-1)
    return joined.astype(jnp.bfloat16)

def prefill_block(query_block, block_index, latent, block_mask):
    query_wide = query_block.astype(jnp.float32)
    query_pos = block_index * BLK + jnp.arange(BLK, dtype=jnp.int32)

    def absorb(carried, key_block):
        running_max, running_sum, weighted = carried
        key_rows = lax.dynamic_slice_in_dim(latent, key_block * BLK, BLK, 0).astype(jnp.float32)
        key_pos = key_block * BLK + jnp.arange(BLK, dtype=jnp.int32)
        allowed = key_pos[None, :] <= query_pos[:, None]
        scores = jnp.einsum('thc,sc->ths', query_wide, key_rows) * scale_factor
        scores = jnp.where(allowed[:, None, :], scores, neg_large)
        new_max = jnp.maximum(running_max, lax.optimization_barrier(jnp.max(scores, axis=-1)))
        weights = jnp.where(allowed[:, None, :], jnp.exp(scores - new_max[..., None]), 0.0)
        factor = jnp.exp(running_max - new_max)
        rounded = lax.optimization_barrier(weights.astype(jnp.bfloat16)).astype(jnp.float32)
        running_sum = running_sum * factor + lax.optimization_barrier(jnp.sum(weights, axis=-1))
        weighted = weighted * factor[..., None] + jnp.einsum('ths,sc->thc', rounded, key_rows[:, :KVR])
        return (new_max, running_sum, weighted)

    def skip_block(carried, key_block):
        return carried

    def visit_block(carried, key_block):
        live = (block_mask[block_index, key_block] == 1) & (key_block <= block_index)
        return (lax.cond(live, absorb, skip_block, carried, key_block), None)
    start_state = (jnp.full((BLK, HEADS), neg_large, jnp.float32), jnp.zeros((BLK, HEADS), jnp.float32), jnp.zeros((BLK, HEADS, KVR), jnp.float32))
    final_state, unused = lax.scan(visit_block, start_state, jnp.arange(NBLK, dtype=jnp.int32))
    return (final_state[2] / final_state[1][..., None]).astype(jnp.bfloat16)

def reference(q_prefill, kv_raw, kv_gain, block_mask, owner, decode_len, q_decode, kv_new_raw):
    latent = normalize_latent(kv_raw, kv_gain, jnp.arange(TOKENS, dtype=jnp.int32))
    query_blocks = q_prefill.reshape(NBLK, BLK, HEADS, LAT)

    def one_block(packed):
        return prefill_block(packed[0], packed[1], latent, block_mask)
    prefill_out = lax.map(one_block, (query_blocks, jnp.arange(NBLK, dtype=jnp.int32))).reshape(TOKENS, HEADS, KVR)
    block_ids = jnp.arange(NBLK, dtype=jnp.int32)
    same_owner = owner[:, None] == owner[None, :]
    earlier = block_ids[None, :] < block_ids[:, None]
    rank = lax.optimization_barrier(jnp.sum((same_owner & earlier).astype(jnp.int32), axis=1)).astype(jnp.int32)
    slot = (owner * CAP + rank).astype(jnp.int32)
    owner_cache = jnp.zeros((SLOTS, BLK, LAT), jnp.bfloat16).at[slot].set(latent.reshape(NBLK, BLK, LAT))
    new_pos = decode_len[None, :] + jnp.arange(STEPS, dtype=jnp.int32)[:, None]
    new_latent = normalize_latent(kv_new_raw, kv_gain, new_pos)
    query_wide = q_decode.astype(jnp.float32)
    cache_scores = jnp.einsum('srhc,uc->srhu', query_wide, latent.astype(jnp.float32)) * scale_factor
    cache_valid = jnp.arange(TOKENS, dtype=jnp.int32)[None, :] < decode_len[:, None]
    cache_scores = jnp.where(cache_valid[None, :, None, :], cache_scores, neg_large)
    new_scores = jnp.einsum('srhc,jrc->srhj', query_wide, new_latent.astype(jnp.float32)) * scale_factor
    new_valid = jnp.arange(STEPS)[None, :] <= jnp.arange(STEPS)[:, None]
    new_scores = jnp.where(new_valid[:, None, None, :], new_scores, neg_large)
    top = jnp.maximum(lax.optimization_barrier(jnp.max(cache_scores, axis=-1)), lax.optimization_barrier(jnp.max(new_scores, axis=-1)))
    cache_weights = jnp.where(cache_valid[None, :, None, :], jnp.exp(cache_scores - top[..., None]), 0.0)
    new_weights = jnp.where(new_valid[:, None, None, :], jnp.exp(new_scores - top[..., None]), 0.0)
    total = lax.optimization_barrier(jnp.sum(cache_weights, axis=-1)) + lax.optimization_barrier(jnp.sum(new_weights, axis=-1))
    cache_rounded = lax.optimization_barrier(cache_weights.astype(jnp.bfloat16)).astype(jnp.float32)
    new_rounded = lax.optimization_barrier(new_weights.astype(jnp.bfloat16)).astype(jnp.float32)
    weighted = jnp.einsum('srhu,uc->srhc', cache_rounded, latent[:, :KVR].astype(jnp.float32))
    weighted = weighted + jnp.einsum('srhj,jrc->srhc', new_rounded, new_latent[..., :KVR].astype(jnp.float32))
    decode_out = (weighted / total[..., None]).astype(jnp.bfloat16)
    return (prefill_out, owner_cache, decode_out)
```

```python
import functools
import math

import jax
import jax.numpy as jnp
from jax import lax
from jax.experimental import pallas as pl
from jax.experimental.pallas import tpu as pltpu
from jax.sharding import PartitionSpec as P

BLK = 128
CAP = 2
SUB = 256
SPAN = 8

scale_factor = 192.0 ** (-0.5)
exponent_scale = scale_factor * math.log2(math.e)
neg_large = -1e30
VMEM_LIMIT = 56 * 1024 * 1024


def frequencies(half):
    lane = lax.broadcasted_iota(jnp.int32, (1, half), 1).astype(jnp.float32)
    return 10000.0 ** (-2.0 * lane / (2 * half))


def normalize_rows(raw, gain, pos, freq):
    width = gain.shape[1]
    half = (raw.shape[1] - width) // 2
    values = raw.astype(jnp.float32)
    main = values[:, :width]
    mean = jnp.mean(main * main, axis=-1, keepdims=True)
    main = main * lax.rsqrt(mean + 1e-06) * gain
    angles = pos.astype(jnp.float32) * freq
    cosine, sine = jnp.cos(angles), jnp.sin(angles)
    first = values[:, width : width + half]
    second = values[:, width + half :]
    return jnp.concatenate(
        [main, first * cosine - second * sine, first * sine + second * cosine], axis=-1
    ).astype(jnp.bfloat16)


def dot_nt(a, b):
    return lax.dot_general(a, b, (((1,), (1,)), ((), ())), preferred_element_type=jnp.float32)


def dot_nn(a, b):
    return lax.dot_general(a, b, (((1,), (0,)), ((), ())), preferred_element_type=jnp.float32)


def weights_of(scores, top):
    return jnp.exp2((scores - top) * exponent_scale)


def prefill_kernel(mask_ref, q_ref, lat_ref, out_ref, keys_ref, count_ref, *, n_blocks, width):
    step = pl.program_id(0)
    me = lax.axis_index("ctx")
    tokens, heads, full = q_ref.shape
    rows = tokens * heads
    span = min(SPAN, n_blocks)

    @pl.when(step == 0)
    def _():
        if n_blocks > span:
            keys_ref[...] = jnp.zeros_like(keys_ref)
        keys_ref[pl.ds(0, BLK), :] = lat_ref[pl.ds(pl.multiple_of(me * BLK, BLK), BLK), :]

        def place(j, count):
            live = (mask_ref[me, j] == 1) & (j < me)

            @pl.when(live)
            def _():
                keys_ref[pl.ds(pl.multiple_of(count * BLK, BLK), BLK), :] = lat_ref[
                    pl.ds(pl.multiple_of(j * BLK, BLK), BLK), :
                ]

            return count + live.astype(jnp.int32)

        count = lax.fori_loop(0, n_blocks, place, jnp.int32(1))
        count_ref[0] = count

        @pl.when(count < n_blocks)
        def _():
            keys_ref[pl.ds(pl.multiple_of(count * BLK, BLK), BLK), :] = jnp.zeros(
                (BLK, full), keys_ref.dtype
            )

    count = count_ref[0]
    live_keys = count * BLK
    n_sub = rows // SUB
    sub_tokens = SUB // heads

    def load_q(i):
        return q_ref[i * sub_tokens : (i + 1) * sub_tokens].reshape(SUB, full)

    def masked(scores, i, base):
        shape = scores.shape
        column = base + lax.broadcasted_iota(jnp.int32, shape, 1)
        token = step * tokens + i * sub_tokens + lax.broadcasted_iota(jnp.int32, shape, 0) // heads
        limit = jnp.where(column < BLK, token + 1, live_keys)
        return jnp.where(column < limit, scores, neg_large)

    def mask_pairs(scores, i):
        n_keys = scores.shape[1]
        parts = []
        row = lax.broadcasted_iota(jnp.int32, (SUB, BLK), 0) // heads
        column = lax.broadcasted_iota(jnp.int32, (SUB, BLK), 1)
        token = step * tokens + i * sub_tokens + row
        parts.append(jnp.where(column <= token, scores[:, :BLK], neg_large))
        if n_keys > 2 * BLK:
            parts.append(scores[:, BLK : n_keys - BLK])
        last = jnp.where(live_keys == n_keys, 0.0, neg_large)
        parts.append(scores[:, n_keys - BLK :] + last)
        return jnp.concatenate(parts, axis=1)

    def store(i, weighted, total):
        result = weighted * (1.0 / total)
        out_ref[i * sub_tokens : (i + 1) * sub_tokens] = result.astype(out_ref.dtype).reshape(
            sub_tokens, heads, width
        )

    if n_blocks <= span and n_blocks % 2 == 0:
        for pairs in range(1, n_blocks // 2 + 1):
            n_keys = pairs * 2 * BLK

            @pl.when((count + 1) // 2 == pairs)
            def _(n_keys=n_keys):
                scores = dot_nt(load_q(0), keys_ref[:n_keys, :])
                for i in range(n_sub):
                    here = mask_pairs(scores, i)
                    if i + 1 < n_sub:
                        scores = dot_nt(load_q(i + 1), keys_ref[:n_keys, :])
                    top = jnp.max(here, axis=-1, keepdims=True)
                    weights = weights_of(here, top)
                    total = jnp.sum(weights, axis=-1, keepdims=True)
                    weighted = dot_nn(weights.astype(jnp.bfloat16), keys_ref[:n_keys, :width])
                    store(i, weighted, total)

    else:
        chunk = span * BLK
        for i in range(n_sub):
            query = load_q(i)

            def absorb(k, carried, i=i, query=query):
                top, total, weighted = carried
                base = pl.multiple_of(k * chunk, chunk)
                rows_here = keys_ref[pl.ds(base, chunk), :]
                scores = masked(dot_nt(query, rows_here), i, base)
                new_top = jnp.maximum(top, jnp.max(scores, axis=-1, keepdims=True))
                weights = weights_of(scores, new_top)
                factor = weights_of(top, new_top)
                total = total * factor + jnp.sum(weights, axis=-1, keepdims=True)
                weighted = weighted * factor + dot_nn(
                    weights.astype(jnp.bfloat16), rows_here[:, :width]
                )
                return new_top, total, weighted

            start = (
                jnp.full((SUB, 1), neg_large, jnp.float32),
                jnp.zeros((SUB, 1), jnp.float32),
                jnp.zeros((SUB, width), jnp.float32),
            )
            top, total, weighted = lax.fori_loop(0, (count + span - 1) // span, absorb, start)
            store(i, weighted, total)


def prefill(q, gathered, block_mask, width):
    row_count, heads, full = q.shape
    n_blocks = gathered.shape[0] // BLK
    tokens = 32
    return pl.pallas_call(
        functools.partial(prefill_kernel, n_blocks=n_blocks, width=width),
        grid=(row_count // tokens,),
        out_shape=jax.ShapeDtypeStruct((row_count, heads, width), jnp.bfloat16),
        in_specs=[
            pl.BlockSpec(memory_space=pltpu.SMEM),
            pl.BlockSpec((tokens, heads, full), lambda i: (i, 0, 0)),
            pl.BlockSpec(gathered.shape, lambda i: (0, 0)),
        ],
        out_specs=pl.BlockSpec((tokens, heads, width), lambda i: (i, 0, 0)),
        scratch_shapes=[
            pltpu.VMEM(gathered.shape, jnp.bfloat16),
            pltpu.SMEM((1,), jnp.int32),
        ],
        compiler_params=pltpu.CompilerParams(vmem_limit_bytes=VMEM_LIMIT),
        name="prefill",
    )(block_mask, q, gathered)


def decode_kernel(
    owner_ref, len_ref, q_ref, lat_ref, new_ref, gain_ref, out_ref, cache_ref, fresh_ref, *, width
):
    s_step, part = pl.program_id(0), pl.program_id(1)
    me = lax.axis_index("ctx")
    _, r_here, heads, full = q_ref.shape
    n_steps, r_all, _ = new_ref.shape
    n_keys = lat_ref.shape[0]
    n_blocks = n_keys // BLK
    n_new = n_steps * r_all

    @pl.when((s_step == 0) & (part == 0))
    def _():
        cache_ref[...] = jnp.zeros_like(cache_ref)

        def place(b, count):
            mine = owner_ref[b] == me

            @pl.when(mine & (count < CAP))
            def _():
                cache_ref[count] = lat_ref[pl.ds(pl.multiple_of(b * BLK, BLK), BLK), :]

            return count + mine.astype(jnp.int32)

        lax.fori_loop(0, n_blocks, place, jnp.int32(0))
        fresh_ref[...] = jnp.zeros_like(fresh_ref)
        row = lax.broadcasted_iota(jnp.int32, (r_all, 1), 0)
        lens = jnp.zeros((r_all, 1), jnp.int32)
        for r in range(r_all):
            lens = jnp.where(row == r, len_ref[r], lens)
        freq = frequencies((full - width) // 2)
        for s in range(n_steps):
            fresh_ref[s * r_all : (s + 1) * r_all, :] = normalize_rows(
                new_ref[s], gain_ref[...], lens + s, freq
            )

    rows = r_here * heads
    sub_r = SUB // heads
    n_sub = rows // SUB

    def load_q(i):
        return q_ref[0, i * sub_r : (i + 1) * sub_r].reshape(SUB, full)

    def row_limits(i):
        row = lax.broadcasted_iota(jnp.int32, (SUB, 1), 0) // heads
        limit = jnp.zeros((SUB, 1), jnp.int32)
        for k in range(sub_r):
            limit = jnp.where(row == k, len_ref[part * r_here + i * sub_r + k], limit)
        return limit

    def fresh_scores(query, i):
        scores = dot_nt(query, fresh_ref[...])
        column = lax.broadcasted_iota(jnp.int32, scores.shape, 1)
        row = lax.broadcasted_iota(jnp.int32, scores.shape, 0) // heads + part * r_here + i * sub_r
        live = (column % r_all == row) & (column // r_all <= s_step) & (column < n_new)
        return jnp.where(live, scores, neg_large)

    def store(i, weighted, total):
        result = weighted * (1.0 / total)
        out_ref[0, i * sub_r : (i + 1) * sub_r] = result.astype(out_ref.dtype).reshape(
            sub_r, heads, width
        )

    def absorb_fresh(query, i):
        scores = fresh_scores(query, i)
        return scores, jnp.max(scores, axis=-1, keepdims=True)

    def cache_scores(query, limit, base, chunk):
        scores = dot_nt(query, lat_ref[pl.ds(base, chunk), :])
        column = base + lax.broadcasted_iota(jnp.int32, scores.shape, 1)
        return jnp.where(column < limit, scores, neg_large)

    chunk = min(SPAN, n_blocks) * BLK
    for i in range(n_sub):
        query = load_q(i)
        limit = row_limits(i)
        extra, top = absorb_fresh(query, i)
        if n_keys == chunk:
            scores = cache_scores(query, limit, 0, chunk)
            top = jnp.maximum(top, jnp.max(scores, axis=-1, keepdims=True))
            weights = weights_of(scores, top)
            extra = weights_of(extra, top)
            total = jnp.sum(weights, axis=-1, keepdims=True) + jnp.sum(
                extra, axis=-1, keepdims=True
            )
            weighted = dot_nn(weights.astype(jnp.bfloat16), lat_ref[:, :width]) + dot_nn(
                extra.astype(jnp.bfloat16), fresh_ref[:, :width]
            )
        else:
            extra = weights_of(extra, top)
            state = (
                top,
                jnp.sum(extra, axis=-1, keepdims=True),
                dot_nn(extra.astype(jnp.bfloat16), fresh_ref[:, :width]),
            )

            def absorb(k, carried, query=query, limit=limit):
                top, total, weighted = carried
                base = pl.multiple_of(k * chunk, chunk)
                scores = cache_scores(query, limit, base, chunk)
                new_top = jnp.maximum(top, jnp.max(scores, axis=-1, keepdims=True))
                weights = weights_of(scores, new_top)
                factor = weights_of(top, new_top)
                total = total * factor + jnp.sum(weights, axis=-1, keepdims=True)
                weighted = weighted * factor + dot_nn(
                    weights.astype(jnp.bfloat16), lat_ref[pl.ds(base, chunk), :width]
                )
                return new_top, total, weighted

            top, total, weighted = lax.fori_loop(0, n_keys // chunk, absorb, state)
        store(i, weighted, total)


def decode(q, gathered, new_raw, gain, owner, decode_len):
    n_steps, r_all, heads, full = q.shape
    width = gain.shape[1]
    n_new = -(-(n_steps * r_all) // BLK) * BLK
    r_here = r_all
    return pl.pallas_call(
        functools.partial(decode_kernel, width=width),
        grid=(n_steps, r_all // r_here),
        out_shape=(
            jax.ShapeDtypeStruct((n_steps, r_all, heads, width), jnp.bfloat16),
            jax.ShapeDtypeStruct((CAP, BLK, full), jnp.bfloat16),
        ),
        in_specs=[
            pl.BlockSpec(memory_space=pltpu.SMEM),
            pl.BlockSpec(memory_space=pltpu.SMEM),
            pl.BlockSpec((1, r_here, heads, full), lambda s, r: (s, r, 0, 0)),
            pl.BlockSpec(gathered.shape, lambda s, r: (0, 0)),
            pl.BlockSpec(new_raw.shape, lambda s, r: (0, 0, 0)),
            pl.BlockSpec(gain.shape, lambda s, r: (0, 0)),
        ],
        out_specs=(
            pl.BlockSpec((1, r_here, heads, width), lambda s, r: (s, r, 0, 0)),
            pl.BlockSpec((CAP, BLK, full), lambda s, r: (0, 0, 0)),
        ),
        scratch_shapes=[pltpu.VMEM((n_new, full), jnp.bfloat16)],
        compiler_params=pltpu.CompilerParams(vmem_limit_bytes=VMEM_LIMIT),
        name="decode",
    )(owner, decode_len, q, gathered, new_raw, gain)


def gather(kv_raw, gain):
    row_count, full = kv_raw.shape
    me = lax.axis_index("ctx")
    positions = me * row_count + jnp.arange(row_count, dtype=jnp.int32)
    freq = frequencies((full - gain.shape[1]) // 2)
    latent = normalize_rows(kv_raw, gain, positions[:, None], freq)
    return lax.all_gather(latent, "ctx", axis=0, tiled=True)


def body(q_prefill, kv_raw, kv_gain, block_mask, owner, decode_len, q_decode, kv_new_raw):
    gain = kv_gain.reshape(1, -1)
    gathered = gather(kv_raw, gain)
    prefill_out = prefill(q_prefill, gathered, block_mask, gain.shape[1])
    decode_out, owner_cache = decode(q_decode, gathered, kv_new_raw, gain, owner, decode_len)
    return (prefill_out, owner_cache, decode_out)


def solution(mesh):
    return jax.shard_map(
        body,
        mesh=mesh,
        in_specs=(
            P(("groups", "ctx"), "head", None),
            P(("groups", "ctx"), None),
            P(),
            P("groups", None),
            P("groups"),
            P("groups"),
            P(None, "groups", "head", None),
            P(None, "groups", None),
        ),
        out_specs=(
            P(("groups", "ctx"), "head", None),
            P(("groups", "ctx"), None, None),
            P(None, "groups", "head", None),
        ),
        check_vma=False,
    )
```

```python
import functools
import math

import jax
import jax.numpy as jnp
from jax import lax
from jax.experimental import pallas as pl
from jax.experimental.pallas import tpu as pltpu
from jax.sharding import PartitionSpec as P

BLK = 128
CAP = 2
SUB = 256
SPAN = 8

scale_factor = 192.0 ** (-0.5)
exponent_scale = scale_factor * math.log2(math.e)
neg_large = -1e30
VMEM_LIMIT = 56 * 1024 * 1024


def frequencies(half):
    lane = lax.broadcasted_iota(jnp.int32, (1, half), 1).astype(jnp.float32)
    return 10000.0 ** (-2.0 * lane / (2 * half))


def normalize_rows(raw, gain, pos, freq):
    width = gain.shape[1]
    half = (raw.shape[1] - width) // 2
    values = raw.astype(jnp.float32)
    main = values[:, :width]
    mean = jnp.mean(main * main, axis=-1, keepdims=True)
    main = main * lax.rsqrt(mean + 1e-06) * gain
    angles = pos.astype(jnp.float32) * freq
    cosine, sine = jnp.cos(angles), jnp.sin(angles)
    first = values[:, width : width + half]
    second = values[:, width + half :]
    return jnp.concatenate(
        [main, first * cosine - second * sine, first * sine + second * cosine], axis=-1
    ).astype(jnp.bfloat16)


def dot_nt(a, b):
    return lax.dot_general(a, b, (((1,), (1,)), ((), ())), preferred_element_type=jnp.float32)


def dot_nn(a, b):
    return lax.dot_general(a, b, (((1,), (0,)), ((), ())), preferred_element_type=jnp.float32)


def weights_of(scores, top):
    return jnp.exp2((scores - top) * exponent_scale)


def prefill_kernel(
    mask_ref, q_ref, keys_ref, flat_ref, out_ref, rows_ref, cols_ref, held_ref, count_ref, *, span
):
    group, step = pl.program_id(0), pl.program_id(1)
    me = lax.axis_index("ctx")
    heads_here, full, tokens = q_ref.shape
    width = out_ref.shape[2]
    group_heads = out_ref.shape[1]
    n_blocks = keys_ref.shape[0]

    @pl.when((group == 0) & (step == 0))
    def _():
        def put(position, block):
            rows_ref[position] = keys_ref[block]
            cols_ref[position] = flat_ref[block, :width, :]

        put(0, me)

        def place(j, count):
            live = (mask_ref[me, j] == 1) & (j < me)

            @pl.when(live)
            def _():
                put(count, j)

            return count + live.astype(jnp.int32)

        count = lax.fori_loop(0, n_blocks, place, jnp.int32(1))
        count_ref[0] = count

        def clear(position, carried):
            rows_ref[position] = jnp.zeros((BLK, full), rows_ref.dtype)
            cols_ref[position] = jnp.zeros((width, BLK), cols_ref.dtype)
            return carried

        lax.fori_loop(count, n_blocks, clear, 0)

    count = count_ref[0]
    pairs_here = heads_here // 2

    def load_q(i):
        return jnp.concatenate([q_ref[2 * i], q_ref[2 * i + 1]], axis=1)

    def scores_of(query, first, blocks):
        rows = rows_ref[pl.ds(first, blocks)].reshape(blocks * BLK, full)
        return dot_nn(rows, query)

    def values_of(first, blocks):
        return jnp.concatenate([cols_ref[first + k] for k in range(blocks)], axis=1)

    row = lax.broadcasted_iota(jnp.int32, (BLK, 2 * tokens), 0)
    token = lax.broadcasted_iota(jnp.int32, (BLK, 2 * tokens), 1) % tokens
    causal = row <= token

    def masked(scores, first, blocks, check_all):
        parts = []
        for k in range(blocks):
            part = scores[k * BLK : (k + 1) * BLK]
            if check_all:
                allowed = jnp.where(first + k == 0, token + 1, jnp.where(first + k < count, BLK, 0))
                part = jnp.where(row < allowed, part, neg_large)
            elif k == 0:
                part = jnp.where(causal, part, neg_large)
            elif k == blocks - 1:
                part = part + jnp.where(count == blocks, 0.0, neg_large)
            parts.append(part)
        return jnp.concatenate(parts, axis=0)

    def store(i, weighted, total):
        result = (weighted * (1.0 / total)).T
        for k in range(2):
            head = step * heads_here + 2 * i + k
            for c in range(width // 128):
                held_ref[c, pl.ds(head, tokens, stride=group_heads), :] = result[
                    k * tokens : (k + 1) * tokens, c * 128 : (c + 1) * 128
                ]

    if n_blocks == span and span % 2 == 0:
        for blocks in range(2, n_blocks + 1, 2):

            @pl.when((count + 1) // 2 * 2 == blocks)
            def _(blocks=blocks):
                scores = scores_of(load_q(0), 0, blocks)
                for i in range(pairs_here):
                    here = masked(scores, 0, blocks, False)
                    if i + 1 < pairs_here:
                        scores = scores_of(load_q(i + 1), 0, blocks)
                    top = jnp.max(here, axis=0, keepdims=True)
                    weights = weights_of(here, top)
                    total = jnp.sum(weights, axis=0, keepdims=True)
                    weighted = dot_nn(values_of(0, blocks), weights.astype(jnp.bfloat16))
                    store(i, weighted, total)

    else:
        for i in range(pairs_here):
            query = load_q(i)

            def absorb(k, carried, query=query):
                top, total, weighted = carried
                scores = masked(scores_of(query, k * span, span), k * span, span, True)
                new_top = jnp.maximum(top, jnp.max(scores, axis=0, keepdims=True))
                weights = weights_of(scores, new_top)
                factor = weights_of(top, new_top)
                total = total * factor + jnp.sum(weights, axis=0, keepdims=True)
                weighted = weighted * factor + dot_nn(
                    values_of(k * span, span), weights.astype(jnp.bfloat16)
                )
                return new_top, total, weighted

            start = (
                jnp.full((1, 2 * tokens), neg_large, jnp.float32),
                jnp.zeros((1, 2 * tokens), jnp.float32),
                jnp.zeros((width, 2 * tokens), jnp.float32),
            )
            top, total, weighted = lax.fori_loop(0, (count + span - 1) // span, absorb, start)
            store(i, weighted, total)

    @pl.when(step == pl.num_programs(1) - 1)
    def _():
        for c in range(width // 128):
            piece = held_ref[c].astype(out_ref.dtype).reshape(tokens, group_heads, 128)
            out_ref[:, :, c * 128 : (c + 1) * 128] = piece


def prefill(q, keys, flat, block_mask, width):
    row_count, heads, full = q.shape
    n_blocks = keys.shape[0]
    group_heads, step_heads = 16, 4
    steps = group_heads // step_heads
    whole = lambda g, i: (0, 0, 0)
    return pl.pallas_call(
        functools.partial(prefill_kernel, span=min(SPAN, n_blocks)),
        grid=(heads // group_heads, steps),
        out_shape=jax.ShapeDtypeStruct((row_count, heads, width), jnp.bfloat16),
        in_specs=[
            pl.BlockSpec(memory_space=pltpu.SMEM),
            pl.BlockSpec((step_heads, full, row_count), lambda g, i: (g * steps + i, 0, 0)),
            pl.BlockSpec(keys.shape, whole, pipeline_mode=pl.Buffered(1)),
            pl.BlockSpec(flat.shape, whole, pipeline_mode=pl.Buffered(1)),
        ],
        out_specs=pl.BlockSpec((row_count, group_heads, width), lambda g, i: (0, g, 0)),
        scratch_shapes=[
            pltpu.VMEM(keys.shape, jnp.bfloat16),
            pltpu.VMEM((n_blocks, width, BLK), jnp.bfloat16),
            pltpu.VMEM((width // 128, row_count * group_heads, 128), jnp.float32),
            pltpu.SMEM((1,), jnp.int32),
        ],
        compiler_params=pltpu.CompilerParams(vmem_limit_bytes=VMEM_LIMIT),
        name="prefill",
    )(block_mask, q.transpose(1, 2, 0), keys, flat)


def decode_kernel(
    owner_ref, len_ref, q_ref, lat_ref, flat_ref, new_ref, gain_ref, out_ref, cache_ref, fresh_ref, *, width
):
    s_step, part = pl.program_id(0), pl.program_id(1)
    me = lax.axis_index("ctx")
    _, r_here, heads, full = q_ref.shape
    n_steps, r_all, _ = new_ref.shape
    n_blocks = lat_ref.shape[0]
    n_keys = n_blocks * BLK
    n_new = n_steps * r_all

    @pl.when((s_step == 0) & (part == 0))
    def _():
        cache_ref[...] = jnp.zeros_like(cache_ref)

        def place(b, count):
            mine = owner_ref[b] == me

            @pl.when(mine & (count < CAP))
            def _():
                cache_ref[count] = flat_ref[b]

            return count + mine.astype(jnp.int32)

        lax.fori_loop(0, n_blocks, place, jnp.int32(0))
        fresh_ref[...] = jnp.zeros_like(fresh_ref)
        row = lax.broadcasted_iota(jnp.int32, (r_all, 1), 0)
        lens = jnp.zeros((r_all, 1), jnp.int32)
        for r in range(r_all):
            lens = jnp.where(row == r, len_ref[r], lens)
        freq = frequencies((full - width) // 2)
        for s in range(n_steps):
            fresh_ref[s * r_all : (s + 1) * r_all, :] = normalize_rows(
                new_ref[s], gain_ref[...], lens + s, freq
            )

    rows = r_here * heads
    sub_r = SUB // heads
    n_sub = rows // SUB

    def load_q(i):
        return q_ref[0, i * sub_r : (i + 1) * sub_r].reshape(SUB, full)

    def row_limits(i):
        row = lax.broadcasted_iota(jnp.int32, (SUB, 1), 0) // heads
        limit = jnp.zeros((SUB, 1), jnp.int32)
        for k in range(sub_r):
            limit = jnp.where(row == k, len_ref[part * r_here + i * sub_r + k], limit)
        return limit

    def fresh_scores(query, i):
        scores = dot_nt(query, fresh_ref[...])
        column = lax.broadcasted_iota(jnp.int32, scores.shape, 1)
        row = lax.broadcasted_iota(jnp.int32, scores.shape, 0) // heads + part * r_here + i * sub_r
        live = (column % r_all == row) & (column // r_all <= s_step) & (column < n_new)
        return jnp.where(live, scores, neg_large)

    def store(i, weighted, total):
        result = weighted * (1.0 / total)
        out_ref[0, i * sub_r : (i + 1) * sub_r] = result.astype(out_ref.dtype).reshape(
            sub_r, heads, width
        )

    def absorb_fresh(query, i):
        scores = fresh_scores(query, i)
        return scores, jnp.max(scores, axis=-1, keepdims=True)

    def cache_scores(query, limit, first, blocks):
        flat = jnp.concatenate([flat_ref[first + k] for k in range(blocks)], axis=1)
        scores = dot_nn(query, flat)
        column = first * BLK + lax.broadcasted_iota(jnp.int32, scores.shape, 1)
        return jnp.where(column < limit, scores, neg_large)

    span = min(SPAN, n_blocks)

    def values_of(first):
        return lat_ref[pl.ds(first, span), :, :width].reshape(span * BLK, width)

    def open_tile(i):
        query = load_q(i)
        extra, top = absorb_fresh(query, i)
        limit = row_limits(i)
        scores = cache_scores(query, limit, 0, span)
        return query, limit, extra, jnp.maximum(top, jnp.max(scores, axis=-1, keepdims=True)), scores

    tile = open_tile(0)
    for i in range(n_sub):
        query, limit, extra, top, scores = tile
        if i + 1 < n_sub:
            tile = open_tile(i + 1)
        weights = weights_of(scores, top)
        extra = weights_of(extra, top)
        total = jnp.sum(weights, axis=-1, keepdims=True) + jnp.sum(extra, axis=-1, keepdims=True)
        weighted = dot_nn(weights.astype(jnp.bfloat16), values_of(0)) + dot_nn(
            extra.astype(jnp.bfloat16), fresh_ref[:, :width]
        )
        if n_blocks > span:

            def absorb(k, carried, query=query, limit=limit):
                top, total, weighted = carried
                scores = cache_scores(query, limit, k * span, span)
                new_top = jnp.maximum(top, jnp.max(scores, axis=-1, keepdims=True))
                weights = weights_of(scores, new_top)
                factor = weights_of(top, new_top)
                total = total * factor + jnp.sum(weights, axis=-1, keepdims=True)
                weighted = weighted * factor + dot_nn(
                    weights.astype(jnp.bfloat16), values_of(k * span)
                )
                return new_top, total, weighted

            top, total, weighted = lax.fori_loop(
                1, n_blocks // span, absorb, (top, total, weighted)
            )
        store(i, weighted, total)


def decode(q, keys, flat, new_raw, gain, owner, decode_len):
    n_steps, r_all, heads, full = q.shape
    width = gain.shape[1]
    n_new = -(-(n_steps * r_all) // BLK) * BLK
    r_here = r_all
    return pl.pallas_call(
        functools.partial(decode_kernel, width=width),
        grid=(n_steps, r_all // r_here),
        out_shape=(
            jax.ShapeDtypeStruct((n_steps, r_all, heads, width), jnp.bfloat16),
            jax.ShapeDtypeStruct((CAP, full, BLK), jnp.bfloat16),
        ),
        in_specs=[
            pl.BlockSpec(memory_space=pltpu.SMEM),
            pl.BlockSpec(memory_space=pltpu.SMEM),
            pl.BlockSpec((1, r_here, heads, full), lambda s, r: (s, r, 0, 0)),
            pl.BlockSpec(keys.shape, lambda s, r: (0, 0, 0), pipeline_mode=pl.Buffered(1)),
            pl.BlockSpec(flat.shape, lambda s, r: (0, 0, 0), pipeline_mode=pl.Buffered(1)),
            pl.BlockSpec(new_raw.shape, lambda s, r: (0, 0, 0)),
            pl.BlockSpec(gain.shape, lambda s, r: (0, 0)),
        ],
        out_specs=(
            pl.BlockSpec((1, r_here, heads, width), lambda s, r: (s, r, 0, 0)),
            pl.BlockSpec((CAP, full, BLK), lambda s, r: (0, 0, 0)),
        ),
        scratch_shapes=[pltpu.VMEM((n_new, full), jnp.bfloat16)],
        compiler_params=pltpu.CompilerParams(vmem_limit_bytes=VMEM_LIMIT),
        name="decode",
    )(owner, decode_len, q, keys, flat, new_raw, gain)


def gather_kernel(
    raw_ref, gain_ref, flat_ref, keys_ref,
    near_send, near_recv, row_send, row_recv, core_send, core_recv, *, n_ctx, minor,
):
    me = lax.axis_index("ctx")
    core = lax.axis_index("head")
    full, tokens = raw_ref.shape
    width = gain_ref.shape[1]
    half = (full - width) // 2
    share = full // 2
    n_major = n_ctx // minor
    my_major, my_minor = me // minor, me % minor

    def at(major_step, minor_step):
        return lax.rem(my_major + major_step, n_major) * minor + lax.rem(my_minor + minor_step, minor)

    def tell(device):
        pl.semaphore_signal(barrier, inc=1, device_id=device, device_id_type=pl.DeviceIdType.MESH)

    barrier = pltpu.get_barrier_semaphore()
    for k in range(1, n_major):
        tell({"ctx": at(k, 0)})
    for k in range(1, minor):
        tell({"ctx": at(0, k)})
    tell({"head": 1 - core})

    values = raw_ref[...].astype(jnp.float32)
    main = values[:width]
    gain = jnp.broadcast_to(gain_ref[...], (tokens, width)).T
    main = main * lax.rsqrt(jnp.mean(main * main, axis=0, keepdims=True) + 1e-06) * gain
    index = lax.broadcasted_iota(jnp.int32, (half, tokens), 0).astype(jnp.float32)
    place = me * tokens + lax.broadcasted_iota(jnp.int32, (half, tokens), 1)
    angles = place.astype(jnp.float32) * 10000.0 ** (-2.0 * index / (2 * half))
    cosine, sine = jnp.cos(angles), jnp.sin(angles)
    first, second = values[width : width + half], values[width + half :]
    flat_ref[me] = jnp.concatenate(
        [main, first * cosine - second * sine, first * sine + second * cosine], axis=0
    ).astype(jnp.bfloat16)

    pl.semaphore_wait(barrier, n_major + minor - 1)

    def copy(block, device, send, recv, of_core=None):
        begin = pl.multiple_of((core if of_core is None else of_core) * share, share)
        piece = flat_ref.at[block, pl.ds(begin, share), :]
        return pltpu.make_async_remote_copy(
            src_ref=piece, dst_ref=piece, send_sem=send, recv_sem=recv,
            device_id=device, device_id_type=pl.DeviceIdType.MESH,
        )

    started = []

    def start(transfer):
        transfer.start()
        started.append(transfer)

    def along_row(k):
        for j in range(1, minor):
            start(copy(at(n_major - k, 0), {"ctx": at(0, j)}, row_send.at[k, j], row_recv.at[k, j]))

    def to_core(k, j):
        block = at(lax.rem(n_major - k, n_major), lax.rem(minor - j, minor))
        start(copy(block, {"head": 1 - core}, core_send.at[k, j], core_recv.at[k, j]))

    along_row(0)
    for k in range(1, n_major):
        start(copy(me, {"ctx": at(k, 0)}, near_send.at[k], near_recv.at[k]))
    keys_ref[me] = flat_ref[me].T

    def arrived(block, recv, of_core=None):
        copy(block, {"head": 1 - core}, recv, recv, of_core).wait_recv()

    def row_arrivals(k):
        for j in range(1, minor):
            arrived(at(n_major - k, minor - j), row_recv.at[k, j])
            to_core(k, j)

    for k in range(1, n_major):
        arrived(at(n_major - k, 0), near_recv.at[k])
        along_row(k)
        to_core(k, 0)
        row_arrivals(k - 1)
    row_arrivals(n_major - 1)
    for k in range(n_major):
        for j in range(minor):
            if k or j:
                block = at(n_major - k, minor - j)
                arrived(block, core_recv.at[k, j], 1 - core)
                keys_ref[block] = flat_ref[block].T
    for transfer in started:
        transfer.wait_send()


def gather(kv_raw, gain, n_ctx):
    row_count, full = kv_raw.shape
    minor = 2 ** (int(math.log2(n_ctx)) // 2)
    n_major = n_ctx // minor
    sems = [pltpu.SemaphoreType.DMA((n_major,))] * 2 + [pltpu.SemaphoreType.DMA((n_major, minor))] * 4
    return pl.pallas_call(
        functools.partial(gather_kernel, n_ctx=n_ctx, minor=minor),
        out_shape=(
            jax.ShapeDtypeStruct((n_ctx, full, row_count), jnp.bfloat16),
            jax.ShapeDtypeStruct((n_ctx, row_count, full), jnp.bfloat16),
        ),
        in_specs=[pl.BlockSpec(memory_space=pltpu.VMEM)] * 2,
        out_specs=(pl.BlockSpec(memory_space=pltpu.VMEM),) * 2,
        scratch_shapes=sems,
        compiler_params=pltpu.CompilerParams(
            collective_id=0, has_side_effects=True, vmem_limit_bytes=VMEM_LIMIT
        ),
        name="gather",
    )(kv_raw.T, gain)


def body(n_ctx, q_prefill, kv_raw, kv_gain, block_mask, owner, decode_len, q_decode, kv_new_raw):
    gain = kv_gain.reshape(1, -1)
    flat, keys = gather(kv_raw, gain, n_ctx)
    prefill_out = prefill(q_prefill, keys, flat, block_mask, gain.shape[1])
    decode_out, cache = decode(q_decode, keys, flat, kv_new_raw, gain, owner, decode_len)
    return (prefill_out, cache.transpose(0, 2, 1), decode_out)


def solution(mesh):
    return jax.shard_map(
        functools.partial(body, mesh.shape["ctx"]),
        mesh=mesh,
        in_specs=(
            P(("groups", "ctx"), "head", None),
            P(("groups", "ctx"), None),
            P(),
            P("groups", None),
            P("groups"),
            P("groups"),
            P(None, "groups", "head", None),
            P(None, "groups", None),
        ),
        out_specs=(
            P(("groups", "ctx"), "head", None),
            P(("groups", "ctx"), None, None),
            P(None, "groups", "head", None),
        ),
        check_vma=False,
    )
```

```python
import functools
import math

import jax
import jax.numpy as jnp
from jax import lax
from jax.experimental import pallas as pl
from jax.experimental.pallas import tpu as pltpu
from jax.sharding import PartitionSpec as P

BLK = 128
CAP = 2
SUB = 256
SPAN = 8

scale_factor = 192.0 ** (-0.5)
exponent_scale = scale_factor * math.log2(math.e)
neg_large = -1e30


def vmem_limit(n_blocks):
    return (40 if n_blocks <= SPAN else 56) * 1024 * 1024


def frequencies(half):
    lane = lax.broadcasted_iota(jnp.int32, (1, half), 1).astype(jnp.float32)
    return 10000.0 ** (-2.0 * lane / (2 * half))


def normalize_rows(raw, gain, pos, freq):
    width = gain.shape[1]
    half = (raw.shape[1] - width) // 2
    values = raw.astype(jnp.float32)
    main = values[:, :width]
    mean = jnp.mean(main * main, axis=-1, keepdims=True)
    main = main * lax.rsqrt(mean + 1e-06) * gain
    angles = pos.astype(jnp.float32) * freq
    cosine, sine = jnp.cos(angles), jnp.sin(angles)
    first = values[:, width : width + half]
    second = values[:, width + half :]
    return jnp.concatenate(
        [main, first * cosine - second * sine, first * sine + second * cosine], axis=-1
    ).astype(jnp.bfloat16)


def split_index(x, n):
    if n & (n - 1) == 0:
        return x >> (n.bit_length() - 1), x & (n - 1)
    return x // n, x % n


def dot_nt(a, b):
    return lax.dot_general(a, b, (((1,), (1,)), ((), ())), preferred_element_type=jnp.float32)


def dot_nn(a, b):
    return lax.dot_general(a, b, (((1,), (0,)), ((), ())), preferred_element_type=jnp.float32)


def weights_of(scores, top):
    return jnp.exp2((scores - top) * exponent_scale)


def prefill_kernel(
    mask_ref, q_ref, keys_ref, flat_ref, out_ref, rows_ref, cols_ref, held_ref, count_ref, *, span
):
    group, step = pl.program_id(0), pl.program_id(1)
    me = lax.axis_index("ctx")
    heads_here, full, tokens = q_ref.shape
    width = out_ref.shape[2]
    group_heads = out_ref.shape[1]
    n_blocks = keys_ref.shape[0]

    @pl.when((group == 0) & (step == 0))
    def _():
        def put(position, block):
            rows_ref[position] = keys_ref[block]
            cols_ref[position] = flat_ref[block, :width, :]

        put(0, me)

        def place(j, count):
            live = (mask_ref[me, j] == 1) & (j < me)

            @pl.when(live)
            def _():
                put(count, j)

            return count + live.astype(jnp.int32)

        count = lax.fori_loop(0, n_blocks, place, jnp.int32(1))
        count_ref[0] = count

        def clear(position, carried):
            rows_ref[position] = jnp.zeros((BLK, full), rows_ref.dtype)
            cols_ref[position] = jnp.zeros((width, BLK), cols_ref.dtype)
            return carried

        lax.fori_loop(count, n_blocks, clear, 0)

    count = count_ref[0]
    pairs_here = heads_here // 2

    def load_q(i):
        return jnp.concatenate([q_ref[2 * i], q_ref[2 * i + 1]], axis=1)

    def scores_of(query, first, blocks):
        rows = rows_ref[pl.ds(first, blocks)].reshape(blocks * BLK, full)
        return dot_nn(rows, query)

    def values_of(first, blocks):
        return jnp.concatenate([cols_ref[first + k] for k in range(blocks)], axis=1)

    row = lax.broadcasted_iota(jnp.int32, (BLK, 2 * tokens), 0)
    token = split_index(lax.broadcasted_iota(jnp.int32, (BLK, 2 * tokens), 1), tokens)[1]
    causal = row <= token

    def masked(scores, first, blocks, check_all):
        parts = []
        for k in range(blocks):
            part = scores[k * BLK : (k + 1) * BLK]
            if check_all:
                allowed = jnp.where(first + k == 0, token + 1, jnp.where(first + k < count, BLK, 0))
                part = jnp.where(row < allowed, part, neg_large)
            elif k == 0:
                part = jnp.where(causal, part, neg_large)
            elif k == blocks - 1:
                part = part + jnp.where(count == blocks, 0.0, neg_large)
            parts.append(part)
        return jnp.concatenate(parts, axis=0)

    def store(i, weighted, total):
        result = (weighted * (1.0 / total)).T
        for k in range(2):
            head = step * heads_here + 2 * i + k
            for c in range(width // 128):
                held_ref[c, pl.ds(head, tokens, stride=group_heads), :] = result[
                    k * tokens : (k + 1) * tokens, c * 128 : (c + 1) * 128
                ]

    if n_blocks == span and span % 2 == 0:
        for blocks in range(2, n_blocks + 1, 2):

            @pl.when((count + 1) // 2 * 2 == blocks)
            def _(blocks=blocks):
                scores = scores_of(load_q(0), 0, blocks)
                ready = None
                for i in range(pairs_here):
                    here = masked(scores, 0, blocks, False)
                    if i + 1 < pairs_here:
                        scores = scores_of(load_q(i + 1), 0, blocks)
                    if ready is not None:
                        store(i - 1, dot_nn(values_of(0, blocks), ready[0]), ready[1])
                    top = jnp.max(here, axis=0, keepdims=True)
                    weights = weights_of(here, top)
                    total = jnp.sum(weights, axis=0, keepdims=True)
                    ready = (weights.astype(jnp.bfloat16), total)
                store(pairs_here - 1, dot_nn(values_of(0, blocks), ready[0]), ready[1])

    else:
        for i in range(pairs_here):
            query = load_q(i)

            def absorb(k, carried, query=query):
                top, total, weighted = carried
                scores = masked(scores_of(query, k * span, span), k * span, span, True)
                new_top = jnp.maximum(top, jnp.max(scores, axis=0, keepdims=True))
                weights = weights_of(scores, new_top)
                factor = weights_of(top, new_top)
                total = total * factor + jnp.sum(weights, axis=0, keepdims=True)
                weighted = weighted * factor + dot_nn(
                    values_of(k * span, span), weights.astype(jnp.bfloat16)
                )
                return new_top, total, weighted

            start = (
                jnp.full((1, 2 * tokens), neg_large, jnp.float32),
                jnp.zeros((1, 2 * tokens), jnp.float32),
                jnp.zeros((width, 2 * tokens), jnp.float32),
            )
            top, total, weighted = lax.fori_loop(0, (count + span - 1) // span, absorb, start)
            store(i, weighted, total)

    @pl.when(step == pl.num_programs(1) - 1)
    def _():
        for c in range(width // 128):
            piece = held_ref[c].astype(out_ref.dtype).reshape(tokens, group_heads, 128)
            out_ref[:, :, c * 128 : (c + 1) * 128] = piece


def prefill(q, keys, flat, block_mask, width):
    row_count, heads, full = q.shape
    n_blocks = keys.shape[0]
    group_heads, step_heads = 16, 16
    steps = group_heads // step_heads
    whole = lambda g, i: (0, 0, 0)
    return pl.pallas_call(
        functools.partial(prefill_kernel, span=min(SPAN, n_blocks)),
        grid=(heads // group_heads, steps),
        out_shape=jax.ShapeDtypeStruct((row_count, heads, width), jnp.bfloat16),
        in_specs=[
            pl.BlockSpec(memory_space=pltpu.SMEM),
            pl.BlockSpec((step_heads, full, row_count), lambda g, i: (g * steps + i, 0, 0)),
            pl.BlockSpec(keys.shape, whole, pipeline_mode=pl.Buffered(1)),
            pl.BlockSpec(flat.shape, whole, pipeline_mode=pl.Buffered(1)),
        ],
        out_specs=pl.BlockSpec((row_count, group_heads, width), lambda g, i: (0, g, 0)),
        scratch_shapes=[
            pltpu.VMEM(keys.shape, jnp.bfloat16),
            pltpu.VMEM((n_blocks, width, BLK), jnp.bfloat16),
            pltpu.VMEM((width // 128, row_count * group_heads, 128), jnp.float32),
            pltpu.SMEM((1,), jnp.int32),
        ],
        compiler_params=pltpu.CompilerParams(vmem_limit_bytes=vmem_limit(n_blocks)),
        name="prefill",
    )(block_mask, q.transpose(1, 2, 0), keys, flat)


def decode_kernel(
    owner_ref, len_ref, q_ref, lat_ref, flat_ref, new_ref, gain_ref, out_ref, cache_ref, fresh_ref, *, width
):
    s_step, part = pl.program_id(0), pl.program_id(1)
    me = lax.axis_index("ctx")
    _, r_here, heads, full = q_ref.shape
    n_steps, r_all, _ = new_ref.shape
    n_blocks = lat_ref.shape[0]
    n_keys = n_blocks * BLK
    n_new = n_steps * r_all

    @pl.when((s_step == 0) & (part == 0))
    def _():
        cache_ref[...] = jnp.zeros_like(cache_ref)

        def place(b, count):
            mine = owner_ref[b] == me

            @pl.when(mine & (count < CAP))
            def _():
                cache_ref[count] = flat_ref[b]

            return count + mine.astype(jnp.int32)

        lax.fori_loop(0, n_blocks, place, jnp.int32(0))
        fresh_ref[...] = jnp.zeros_like(fresh_ref)
        row = lax.broadcasted_iota(jnp.int32, (r_all, 1), 0)
        lens = jnp.zeros((r_all, 1), jnp.int32)
        for r in range(r_all):
            lens = jnp.where(row == r, len_ref[r], lens)
        freq = frequencies((full - width) // 2)
        fresh_ref[:n_new, :] = normalize_rows(
            new_ref[...].reshape(n_new, full),
            gain_ref[...],
            jnp.concatenate([lens + k for k in range(n_steps)], axis=0),
            freq,
        )

    rows = r_here * heads
    sub_r = SUB // heads
    n_sub = rows // SUB

    def load_q(i):
        return q_ref[0, i * sub_r : (i + 1) * sub_r].reshape(SUB, full)

    def row_limits(i):
        row = split_index(lax.broadcasted_iota(jnp.int32, (SUB, 1), 0), heads)[0]
        limit = jnp.zeros((SUB, 1), jnp.int32)
        for k in range(sub_r):
            limit = jnp.where(row == k, len_ref[part * r_here + i * sub_r + k], limit)
        return limit

    def fresh_scores(query, i):
        scores = dot_nt(query, fresh_ref[...])
        column = lax.broadcasted_iota(jnp.int32, scores.shape, 1)
        row = split_index(lax.broadcasted_iota(jnp.int32, scores.shape, 0), heads)[0]
        row = row + part * r_here + i * sub_r
        written_at, row_of = split_index(column, r_all)
        live = (row_of == row) & (written_at <= s_step) & (column < n_new)
        return jnp.where(live, scores, neg_large)

    def store(i, weighted, total):
        result = weighted * (1.0 / total)
        out_ref[0, i * sub_r : (i + 1) * sub_r] = result.astype(out_ref.dtype).reshape(
            sub_r, heads, width
        )

    def absorb_fresh(query, i):
        scores = fresh_scores(query, i)
        return scores, jnp.max(scores, axis=-1, keepdims=True)

    def cache_scores(query, limit, first, blocks):
        flat = jnp.concatenate([flat_ref[first + k] for k in range(blocks)], axis=1)
        scores = dot_nn(query, flat)
        column = first * BLK + lax.broadcasted_iota(jnp.int32, scores.shape, 1)
        return jnp.where(column < limit, scores, neg_large)

    span = min(SPAN, n_blocks)

    def values_of(first):
        return lat_ref[pl.ds(first, span), :, :width].reshape(span * BLK, width)

    def open_tile(i):
        query = load_q(i)
        extra, top = absorb_fresh(query, i)
        limit = row_limits(i)
        scores = cache_scores(query, limit, 0, span)
        return query, limit, extra, jnp.maximum(top, jnp.max(scores, axis=-1, keepdims=True)), scores

    tile = open_tile(0)
    for i in range(n_sub):
        query, limit, extra, top, scores = tile
        if i + 1 < n_sub:
            tile = open_tile(i + 1)
        weights = weights_of(scores, top)
        extra = weights_of(extra, top)
        total = jnp.sum(weights, axis=-1, keepdims=True) + jnp.sum(extra, axis=-1, keepdims=True)
        weighted = dot_nn(weights.astype(jnp.bfloat16), values_of(0)) + dot_nn(
            extra.astype(jnp.bfloat16), fresh_ref[:, :width]
        )
        if n_blocks > span:

            def absorb(k, carried, query=query, limit=limit):
                top, total, weighted = carried
                scores = cache_scores(query, limit, k * span, span)
                new_top = jnp.maximum(top, jnp.max(scores, axis=-1, keepdims=True))
                weights = weights_of(scores, new_top)
                factor = weights_of(top, new_top)
                total = total * factor + jnp.sum(weights, axis=-1, keepdims=True)
                weighted = weighted * factor + dot_nn(
                    weights.astype(jnp.bfloat16), values_of(k * span)
                )
                return new_top, total, weighted

            top, total, weighted = lax.fori_loop(
                1, n_blocks // span, absorb, (top, total, weighted)
            )
        store(i, weighted, total)


def decode(q, keys, flat, new_raw, gain, owner, decode_len):
    n_steps, r_all, heads, full = q.shape
    width = gain.shape[1]
    n_new = -(-(n_steps * r_all) // BLK) * BLK
    r_here = r_all
    return pl.pallas_call(
        functools.partial(decode_kernel, width=width),
        grid=(n_steps, r_all // r_here),
        out_shape=(
            jax.ShapeDtypeStruct((n_steps, r_all, heads, width), jnp.bfloat16),
            jax.ShapeDtypeStruct((CAP, full, BLK), jnp.bfloat16),
        ),
        in_specs=[
            pl.BlockSpec(memory_space=pltpu.SMEM),
            pl.BlockSpec(memory_space=pltpu.SMEM),
            pl.BlockSpec((1, r_here, heads, full), lambda s, r: (s, r, 0, 0)),
            pl.BlockSpec(keys.shape, lambda s, r: (0, 0, 0), pipeline_mode=pl.Buffered(1)),
            pl.BlockSpec(flat.shape, lambda s, r: (0, 0, 0), pipeline_mode=pl.Buffered(1)),
            pl.BlockSpec(new_raw.shape, lambda s, r: (0, 0, 0)),
            pl.BlockSpec(gain.shape, lambda s, r: (0, 0)),
        ],
        out_specs=(
            pl.BlockSpec((1, r_here, heads, width), lambda s, r: (s, r, 0, 0)),
            pl.BlockSpec((CAP, full, BLK), lambda s, r: (0, 0, 0)),
        ),
        scratch_shapes=[pltpu.VMEM((n_new, full), jnp.bfloat16)],
        compiler_params=pltpu.CompilerParams(vmem_limit_bytes=vmem_limit(keys.shape[0])),
        name="decode",
    )(owner, decode_len, q, keys, flat, new_raw, gain)


def gather_kernel(
    raw_ref, gain_ref, flat_ref, keys_ref,
    near_send, near_recv, row_send, row_recv, core_send, core_recv, *, n_ctx, minor,
):
    me = lax.axis_index("ctx")
    core = lax.axis_index("head")
    full, tokens = raw_ref.shape
    width = gain_ref.shape[1]
    half = (full - width) // 2
    share = full // 2
    n_major = n_ctx // minor
    my_major, my_minor = me // minor, me % minor

    def at(major_step, minor_step):
        return lax.rem(my_major + major_step, n_major) * minor + lax.rem(my_minor + minor_step, minor)

    def tell(device):
        pl.semaphore_signal(barrier, inc=1, device_id=device, device_id_type=pl.DeviceIdType.MESH)

    barrier = pltpu.get_barrier_semaphore()
    for k in range(1, n_major):
        tell({"ctx": at(k, 0)})
    for k in range(1, minor):
        tell({"ctx": at(0, k)})
    tell({"head": 1 - core})

    values = raw_ref[...].astype(jnp.float32)
    main = values[:width]
    gain = jnp.broadcast_to(gain_ref[...], (tokens, width)).T
    main = main * lax.rsqrt(jnp.mean(main * main, axis=0, keepdims=True) + 1e-06) * gain
    index = lax.broadcasted_iota(jnp.int32, (half, tokens), 0).astype(jnp.float32)
    place = me * tokens + lax.broadcasted_iota(jnp.int32, (half, tokens), 1)
    angles = place.astype(jnp.float32) * 10000.0 ** (-2.0 * index / (2 * half))
    cosine, sine = jnp.cos(angles), jnp.sin(angles)
    first, second = values[width : width + half], values[width + half :]
    flat_ref[me] = jnp.concatenate(
        [main, first * cosine - second * sine, first * sine + second * cosine], axis=0
    ).astype(jnp.bfloat16)

    pl.semaphore_wait(barrier, n_major + minor - 1)

    def copy(block, device, send, recv, of_core=None):
        begin = pl.multiple_of((core if of_core is None else of_core) * share, share)
        piece = flat_ref.at[block, pl.ds(begin, share), :]
        return pltpu.make_async_remote_copy(
            src_ref=piece, dst_ref=piece, send_sem=send, recv_sem=recv,
            device_id=device, device_id_type=pl.DeviceIdType.MESH,
        )

    started = []

    def start(transfer):
        transfer.start()
        started.append(transfer)

    def along_row(k):
        for j in range(1, minor):
            start(copy(at(n_major - k, 0), {"ctx": at(0, j)}, row_send.at[k, j], row_recv.at[k, j]))

    def to_core(k, j):
        block = at(lax.rem(n_major - k, n_major), lax.rem(minor - j, minor))
        start(copy(block, {"head": 1 - core}, core_send.at[k, j], core_recv.at[k, j]))

    along_row(0)
    for k in range(1, n_major):
        start(copy(me, {"ctx": at(k, 0)}, near_send.at[k], near_recv.at[k]))
    keys_ref[me] = flat_ref[me].T

    def arrived(block, recv, of_core=None):
        copy(block, {"head": 1 - core}, recv, recv, of_core).wait_recv()

    def row_arrivals(k):
        for j in range(1, minor):
            arrived(at(n_major - k, minor - j), row_recv.at[k, j])
            to_core(k, j)

    for k in range(1, n_major):
        arrived(at(n_major - k, 0), near_recv.at[k])
        along_row(k)
        to_core(k, 0)
        row_arrivals(k - 1)
    row_arrivals(n_major - 1)
    for k in range(n_major):
        for j in range(minor):
            if k or j:
                block = at(n_major - k, minor - j)
                arrived(block, core_recv.at[k, j], 1 - core)
                keys_ref[block] = flat_ref[block].T
    for transfer in started:
        transfer.wait_send()


def gather(kv_raw, gain, n_ctx):
    row_count, full = kv_raw.shape
    minor = 2 ** (int(math.log2(n_ctx)) // 2)
    n_major = n_ctx // minor
    sems = [pltpu.SemaphoreType.DMA((n_major,))] * 2 + [pltpu.SemaphoreType.DMA((n_major, minor))] * 4
    return pl.pallas_call(
        functools.partial(gather_kernel, n_ctx=n_ctx, minor=minor),
        out_shape=(
            jax.ShapeDtypeStruct((n_ctx, full, row_count), jnp.bfloat16),
            jax.ShapeDtypeStruct((n_ctx, row_count, full), jnp.bfloat16),
        ),
        in_specs=[pl.BlockSpec(memory_space=pltpu.VMEM)] * 2,
        out_specs=(pl.BlockSpec(memory_space=pltpu.VMEM),) * 2,
        scratch_shapes=sems,
        compiler_params=pltpu.CompilerParams(
            collective_id=0, has_side_effects=True, vmem_limit_bytes=vmem_limit(n_ctx)
        ),
        name="gather",
    )(kv_raw.T, gain)


def body(n_ctx, q_prefill, kv_raw, kv_gain, block_mask, owner, decode_len, q_decode, kv_new_raw):
    gain = kv_gain.reshape(1, -1)
    flat, keys = gather(kv_raw, gain, n_ctx)
    prefill_out = prefill(q_prefill, keys, flat, block_mask, gain.shape[1])
    decode_out, cache = decode(q_decode, keys, flat, kv_new_raw, gain, owner, decode_len)
    return (prefill_out, cache.transpose(0, 2, 1), decode_out)


def solution(mesh):
    return jax.shard_map(
        functools.partial(body, mesh.shape["ctx"]),
        mesh=mesh,
        in_specs=(
            P(("groups", "ctx"), "head", None),
            P(("groups", "ctx"), None),
            P(),
            P("groups", None),
            P("groups"),
            P("groups"),
            P(None, "groups", "head", None),
            P(None, "groups", None),
        ),
        out_specs=(
            P(("groups", "ctx"), "head", None),
            P(("groups", "ctx"), None, None),
            P(None, "groups", "head", None),
        ),
        check_vma=False,
    )
```
